256 devices in a mesh: dp: 16 (over y_hi, x, core), tensor: 16 (over y_lo, z).
Axes of the slice: x: 4, y: 4 (y_hi: 2, y_lo: 2; y = y_hi * 2 + y_lo), z: 8, core: 2. Of those that a mesh axis runs over, the one named last changes fastest.
Arguments:
- context: bfloat16 [8192, 4096], P('dp', 'tensor'), parts along dimension 0, may hold values from -6 to 6
- residual_in: bfloat16 [8192, 4096], P(('dp', 'tensor')), parts along dimension 0, may hold values from -6 to 6
- out_weight: bfloat16 [4096, 4096], P('tensor'), may hold values from -0.09375 to 0.09375
- out_bias: float32 [4096], replicated, may hold values from -3 to 3
- norm_gain: float32 [4096], replicated, may hold values from 0.1 to 1.9
- norm_bias: float32 [4096], replicated, may hold values from -3 to 3
- gate_weight: bfloat16 [4096, 8192], P(None, 'tensor'), may hold values from -0.09375 to 0.09375
- up_weight: bfloat16 [4096, 8192], P(None, 'tensor'), may hold values from -0.09375 to 0.09375
Outputs:
- normed: bfloat16 [8192, 4096], P(('dp', 'tensor')), parts along dimension 0
- hidden: bfloat16 [8192, 8192], P('dp', 'tensor'), parts along dimension 0
The draws below stay inside these ranges and needn't reach their ends.
There are 16 independent parts, one for each index of `dp`. The reference program is written for one: setup_inputs(seed, part) draws one part's arguments, and reference() takes and returns one part's arrays. A program takes and returns all parts, laid end to end along the dimension named above; an argument that names none is the same for every part. Nothing has to cross between parts.
All inputs are finite; a program needn't handle non-finite values.
Results may differ from the reference program's by a relative error of at most 0.029.
Values may be sent and summed in bfloat16 or wider, within the bound.
No kernel may reach another device: no remote copies, remote signals or barrier semaphores. Data moves between devices by JAX's collectives and lax.ppermute only.
A program may use at most 64 MiB of HBM per device.

```python
import jax
import jax.numpy as jnp
from jax import lax

D = 4096
FF = 8192
TOKENS = 512
N_TENSOR = 16


def strengthened(result, rng, source, target, parts, factor):
    owner, partner = [(jnp.arange(result.shape[dim]) // (result.shape[dim] // parts)).reshape([-1 if axis == dim else 1 for axis in range(result.ndim)]) for dim in (source, target)]
    chosen = jax.random.permutation(rng, parts)[partner]
    strong = (owner == chosen) | (owner == (partner + parts // 2) % parts)
    return jnp.where(strong, factor * result, result)


def steps_of(own_key, shape, pieces, least, largest):
    def one(axis_at, parts):
        draws = jax.random.uniform(jax.random.fold_in(jax.random.fold_in(own_key, 6), axis_at), (parts,), jnp.float32, least / len(pieces), largest / len(pieces))
        return jnp.repeat(jnp.exp(draws), shape[axis_at] // parts).reshape((-1,) + (1,) * (len(shape) - axis_at - 1))

    gain = one(*pieces[0])
    for cut in pieces[1:]:
        gain = gain * one(*cut)
    return gain


def bell_draw(stream_key, dims, deviation, most, cuts=(), kind=jnp.bfloat16):
    drawn = jax.random.normal(stream_key, dims, jnp.float32) * deviation
    if len(cuts) > 0:
        drawn = steps_of(stream_key, dims, cuts, -0.22, 0.18) * drawn
    return jnp.clip(drawn, min=-most, max=most).astype(kind)


def heavy_noise(own_key, extent, scale, bound, pieces, heavy, kind=jnp.bfloat16):
    values = scale * jax.random.normal(own_key, extent, jnp.float32)
    if pieces:
        values = values * steps_of(own_key, extent, pieces, -0.22, 0.18)
    return jnp.clip(strengthened(values, jax.random.fold_in(own_key, 3), *heavy), -bound, bound).astype(kind)


def setup_inputs(seed: int = 0, part: int = 0) -> dict:
    splits = jax.random.split(jax.random.key(seed), 9)
    own_keys = jax.random.split(jax.random.fold_in(splits[8], part), 9)
    context = heavy_noise(own_keys[0], (TOKENS, D), 1.0, 6.0, ((1, 16),), (1, 0, 16, 2.0))
    residual_in = bell_draw(own_keys[1], (TOKENS, D), 1.0, 6.0, ((0, 16),))
    out_weight = bell_draw(splits[2], (D, D), D ** -0.5, 0.09375, ((0, 16),))
    out_bias = bell_draw(splits[3], (D,), 0.5, 3.0, (), jnp.float32)
    norm_gain = jnp.clip(1.0 + 0.18 * jax.random.normal(splits[4], (D,), jnp.float32), 0.1, 1.9)
    norm_bias = bell_draw(splits[5], (D,), 0.5, 3.0, (), jnp.float32)
    gate_weight = bell_draw(splits[6], (D, FF), D ** -0.5, 0.09375, ((1, 16),))
    up_weight = bell_draw(splits[7], (D, FF), D ** -0.5, 0.09375, ((1, 16),))
    return {"context": context, "residual_in": residual_in, "out_weight": out_weight, "out_bias": out_bias, "norm_gain": norm_gain, "norm_bias": norm_bias, "gate_weight": gate_weight, "up_weight": up_weight}


def reference(context, residual_in, out_weight, out_bias, norm_gain, norm_bias, gate_weight, up_weight):
    width = D // N_TENSOR

    def accumulate(total, index):
        start = (index * width).astype(jnp.int32)
        block = lax.dynamic_slice_in_dim(context, start, width, 1)
        rows = lax.dynamic_slice_in_dim(out_weight, start, width, 0)
        partial_value = jnp.dot(block, rows, preferred_element_type=jnp.float32).astype(jnp.bfloat16)
        partial_value = lax.optimization_barrier(partial_value)
        return (total + partial_value.astype(jnp.float32), None)
    attended, _ = lax.scan(accumulate, jnp.zeros((TOKENS, D), jnp.float32), jnp.arange(N_TENSOR, dtype=jnp.int32))
    stream = residual_in.astype(jnp.float32) + attended + out_bias
    center = lax.optimization_barrier(jnp.mean(stream, axis=1, keepdims=True))
    spread = lax.optimization_barrier(jnp.mean((stream - center) ** 2, axis=1, keepdims=True))
    normed = ((stream - center) / jnp.sqrt(spread + 1e-05) * norm_gain + norm_bias).astype(jnp.bfloat16)
    gate = jnp.dot(normed, gate_weight, preferred_element_type=jnp.float32)
    up = jnp.dot(normed, up_weight, preferred_element_type=jnp.float32)
    hidden = (jax.nn.gelu(gate, approximate=False) * up).astype(jnp.bfloat16)
    return (normed, hidden)
```

```python
import jax
import jax.numpy as jnp
from jax import lax
from jax.sharding import PartitionSpec as P

ROWS = 32
RING = 8
HALF = ROWS // 2


def index_of(y, z):
    return (y % 2) * RING + z % RING


def ring_pairs(step):
    return [(index_of(y, z), index_of(y, z + step)) for y in range(2) for z in range(RING)]


UP, DOWN = ring_pairs(1), ring_pairs(-1)
ACROSS = [(index_of(y, z), index_of(y + 1, z)) for y in range(2) for z in range(RING)]


def send(value, pairs):
    return lax.ppermute(value, "tensor", pairs)


def shards(
    context, residual_in, out_weight, out_bias, norm_gain, norm_bias, gate_weight, up_weight
):
    me = lax.axis_index("tensor")
    y, z = me // RING, me % RING

    def start_of(other, dz):
        return (jnp.bitwise_xor(y, other) * RING + lax.rem(z + dz + RING, RING)) * ROWS

    def partial(*blocks):
        rows = [lax.dynamic_slice_in_dim(context, start_of(*b), ROWS, 0) for b in blocks]
        rows = jnp.concatenate(rows, 0) if len(rows) > 1 else rows[0]
        return jnp.dot(rows, out_weight, preferred_element_type=jnp.float32)

    def bf(value):
        return value.astype(jnp.bfloat16)

    def f32(value):
        return value.astype(jnp.float32)

    far = send(bf(partial((1, 4))), ACROSS)
    side_up = send(bf(partial((1, 2))), UP)
    side_down = send(bf(partial((1, -2))), DOWN)
    three = send(bf(partial((1, 3), (1, -3))), ACROSS)

    total = bf(partial((0, 4)) + f32(far))
    up, down = send(total[:HALF], UP), send(total[HALF:], DOWN)

    side_up = send(bf(partial((1, 1)) + f32(side_up)), UP)
    side_down = send(bf(partial((1, -1)) + f32(side_down)), DOWN)

    pad = jnp.zeros((HALF, up.shape[1]), jnp.bfloat16)
    up = jnp.concatenate([up, pad], 0)
    down = jnp.concatenate([pad, down], 0)
    up = send(bf(partial((0, 3)) + f32(three[:ROWS]) + f32(up)), UP)
    down = send(bf(partial((0, -3)) + f32(three[ROWS:]) + f32(down)), DOWN)

    side = send(bf(partial((1, 0)) + f32(side_up) + f32(side_down)), ACROSS)

    up = send(bf(partial((0, 2)) + f32(up)), UP)
    down = send(bf(partial((0, -2)) + f32(down)), DOWN)
    up = send(bf(partial((0, 1)) + f32(up)), UP)
    down = send(bf(partial((0, -1)) + f32(down)), DOWN)

    attended = partial((0, 0)) + f32(side) + f32(up) + f32(down)

    stream = f32(residual_in) + attended + out_bias
    center = jnp.mean(stream, axis=1, keepdims=True)
    spread = jnp.mean((stream - center) ** 2, axis=1, keepdims=True)
    normed = bf((stream - center) / jnp.sqrt(spread + 1e-05) * norm_gain + norm_bias)

    hidden = jnp.zeros((context.shape[0], gate_weight.shape[1]), jnp.bfloat16)

    def units(hidden, blocks):
        rows = jnp.concatenate([rows for rows, _ in blocks], 0)
        gate = jnp.dot(rows, gate_weight, preferred_element_type=jnp.float32)
        up = jnp.dot(rows, up_weight, preferred_element_type=jnp.float32)
        out = bf(jax.nn.gelu(gate, approximate=False) * up)
        for i, (_, block) in enumerate(blocks):
            hidden = lax.dynamic_update_slice_in_dim(
                hidden, out[i * ROWS : (i + 1) * ROWS], start_of(*block), 0
            )
        return hidden

    up1, down1 = send(normed, UP), send(normed, DOWN)
    other = send(normed, ACROSS)
    up2, down2 = send(up1, UP), send(down1, DOWN)
    side_up1, side_down1 = send(other, UP), send(other, DOWN)
    hidden = units(hidden, [(normed, (0, 0)), (other, (1, 0)), (up1, (0, -1)), (down1, (0, 1))])
    up3, down3 = send(up2, UP), send(down2, DOWN)
    side_up2, side_down2 = send(side_up1, UP), send(side_down1, DOWN)
    hidden = units(
        hidden, [(side_up1, (1, -1)), (side_down1, (1, 1)), (up2, (0, -2)), (down2, (0, 2))]
    )
    up4, down4 = send(up3[:HALF], UP), send(down3[HALF:], DOWN)
    three = send(jnp.concatenate([up3, down3], 0), ACROSS)
    hidden = units(
        hidden, [(side_up2, (1, -2)), (side_down2, (1, 2)), (up3, (0, -3)), (down3, (0, 3))]
    )
    four = jnp.concatenate([up4, down4], 0)
    other_four = send(four, ACROSS)
    hidden = units(
        hidden, [(three[:ROWS], (1, -3)), (three[ROWS:], (1, 3)), (four, (0, 4)), (other_four, (1, 4))]
    )
    return (normed, hidden)


def solution(mesh):
    in_specs = (
        P("dp", "tensor"),
        P(("dp", "tensor"), None),
        P("tensor", None),
        P(),
        P(),
        P(),
        P(None, "tensor"),
        P(None, "tensor"),
    )
    out_specs = (P(("dp", "tensor"), None), P("dp", "tensor"))
    return jax.shard_map(shards, mesh=mesh, in_specs=in_specs, out_specs=out_specs, check_vma=False)
```

```python
import jax
import jax.numpy as jnp
from jax import lax
from jax.sharding import PartitionSpec as P

ROWS = 32
RING = 8
HALF = ROWS // 2


def index_of(y, z):
    return (y % 2) * RING + z % RING


def ring_pairs(step):
    return [(index_of(y, z), index_of(y, z + step)) for y in range(2) for z in range(RING)]


UP, DOWN = ring_pairs(1), ring_pairs(-1)
ACROSS = [(index_of(y, z), index_of(y + 1, z)) for y in range(2) for z in range(RING)]


def send(value, pairs):
    return lax.ppermute(value, "tensor", pairs)


def hold(values):
    return lax.optimization_barrier(values)


def shards(
    context, residual_in, out_weight, out_bias, norm_gain, norm_bias, gate_weight, up_weight
):
    me = lax.axis_index("tensor")
    y, z = me // RING, me % RING

    def start_of(other, dz):
        return (jnp.bitwise_xor(y, other) * RING + lax.rem(z + dz + RING, RING)) * ROWS

    def bf(value):
        return value.astype(jnp.bfloat16)

    def f32(value):
        return value.astype(jnp.float32)

    ring = context.reshape(2, RING, ROWS, -1)
    ring = lax.dynamic_slice_in_dim(jnp.concatenate([ring, ring], 1), z, RING, 1)
    ring = jnp.where(y == 0, ring, ring[::-1])

    def product(*blocks):
        rows = [ring[other, dz % RING] for other, dz in blocks]
        rows = jnp.concatenate(rows, 0) if len(rows) > 1 else rows[0]
        return bf(jnp.dot(rows, out_weight, preferred_element_type=jnp.float32))

    far = product((1, 4))
    far, ring = hold((far, ring))
    far = send(far, ACROSS)
    rest = product((1, 1), (1, -1), (1, 3), (1, -3), (1, 2), (1, -2))
    side_up = send(rest[:ROWS], UP)
    side_down = send(rest[ROWS : 2 * ROWS], DOWN)
    three = send(rest[2 * ROWS : 4 * ROWS], ACROSS)
    two = send(rest[4 * ROWS :], ACROSS)
    ring, rest = hold((ring, rest))
    own4, own0, side0 = product((0, 4)), product((0, 0)), product((1, 0))
    own3, own2, own1 = (product((0, dz), (0, -dz)) for dz in (3, 2, 1))

    far, own4, own3, own2, own1, own0, side0 = hold((far, own4, own3, own2, own1, own0, side0))
    total = bf(f32(own4) + f32(far))
    up, down = send(total[:HALF], UP), send(total[HALF:], DOWN)

    up, down, three, side_up, side_down, own3, side0 = hold(
        (up, down, three, side_up, side_down, own3, side0)
    )
    pad = jnp.zeros((HALF, up.shape[1]), jnp.bfloat16)
    own3 = f32(own3) + f32(three)
    up = send(bf(own3[:ROWS] + f32(jnp.concatenate([up, pad], 0))), UP)
    down = send(bf(own3[ROWS:] + f32(jnp.concatenate([pad, down], 0))), DOWN)
    side = send(bf(f32(side0) + f32(side_up) + f32(side_down)), ACROSS)

    up, down, two, own2 = hold((up, down, two, own2))
    own2 = f32(own2) + f32(two)
    up = send(bf(own2[:ROWS] + f32(up)), UP)
    down = send(bf(own2[ROWS:] + f32(down)), DOWN)

    up, down, own1 = hold((up, down, own1))
    up = send(bf(f32(own1[:ROWS]) + f32(up)), UP)
    down = send(bf(f32(own1[ROWS:]) + f32(down)), DOWN)

    attended = f32(own0) + f32(side) + f32(up) + f32(down)

    stream = f32(residual_in) + attended + out_bias
    center = jnp.mean(stream, axis=1, keepdims=True)
    spread = jnp.mean((stream - center) ** 2, axis=1, keepdims=True)
    normed = bf((stream - center) / jnp.sqrt(spread + 1e-05) * norm_gain + norm_bias)

    hidden = jnp.zeros((context.shape[0], gate_weight.shape[1]), jnp.bfloat16)

    def units(hidden, blocks):
        rows = jnp.concatenate([rows for rows, _ in blocks], 0)
        gate = jnp.dot(rows, gate_weight, preferred_element_type=jnp.float32)
        up = jnp.dot(rows, up_weight, preferred_element_type=jnp.float32)
        out = bf(jax.nn.gelu(gate, approximate=False) * up)
        for i, (_, block) in enumerate(blocks):
            hidden = lax.dynamic_update_slice_in_dim(
                hidden, out[i * ROWS : (i + 1) * ROWS], start_of(*block), 0
            )
        return hidden

    up1, down1 = send(normed, UP), send(normed, DOWN)
    other = send(normed, ACROSS)
    up1, down1, other, normed = hold((up1, down1, other, normed))

    up2, down2 = send(up1, UP), send(down1, DOWN)
    side_up1, side_down1 = send(other, UP), send(other, DOWN)
    up2, down2, up1, down1, other, normed = hold((up2, down2, up1, down1, other, normed))

    up3, down3 = send(up2, UP), send(down2, DOWN)
    two = send(jnp.concatenate([up2, down2], 0), ACROSS)
    hidden = units(
        hidden, [(normed, (0, 0)), (other, (1, 0)), (up1, (0, -1)), (down1, (0, 1))]
    )
    up3, down3, side_up1, side_down1, up2, down2, hidden, normed = hold(
        (up3, down3, side_up1, side_down1, up2, down2, hidden, normed)
    )

    up4, down4 = send(up3[:HALF], UP), send(down3[HALF:], DOWN)
    three = send(jnp.concatenate([up3, down3], 0), ACROSS)
    hidden = units(
        hidden, [(side_up1, (1, -1)), (side_down1, (1, 1)), (up2, (0, -2)), (down2, (0, 2))]
    )
    up4, down4, up3, down3, hidden = hold((up4, down4, up3, down3, hidden))

    four = jnp.concatenate([up4, down4], 0)
    other_four = send(four, ACROSS)
    two, up3, down3, hidden = hold((two, up3, down3, hidden))
    hidden = units(
        hidden, [(two[:ROWS], (1, -2)), (two[ROWS:], (1, 2)), (up3, (0, -3)), (down3, (0, 3))]
    )
    hidden = units(
        hidden, [(three[:ROWS], (1, -3)), (three[ROWS:], (1, 3)), (four, (0, 4)), (other_four, (1, 4))]
    )
    return (normed, hidden)


def solution(mesh):
    in_specs = (
        P("dp", "tensor"),
        P(("dp", "tensor"), None),
        P("tensor", None),
        P(),
        P(),
        P(),
        P(None, "tensor"),
        P(None, "tensor"),
    )
    out_specs = (P(("dp", "tensor"), None), P("dp", "tensor"))
    return jax.shard_map(shards, mesh=mesh, in_specs=in_specs, out_specs=out_specs, check_vma=False)
```

```python
import jax
import jax.numpy as jnp
from jax import lax
from jax.sharding import PartitionSpec as P

ROWS = 32
RING = 8
HALF = ROWS // 2


def index_of(y, z):
    return (y % 2) * RING + z % RING


def ring_pairs(step):
    return [(index_of(y, z), index_of(y, z + step)) for y in range(2) for z in range(RING)]


UP, DOWN = ring_pairs(1), ring_pairs(-1)
ACROSS = [(index_of(y, z), index_of(y + 1, z)) for y in range(2) for z in range(RING)]


def send(value, pairs):
    return lax.ppermute(value, "tensor", pairs)


def hold(values):
    return lax.optimization_barrier(values)


def shards(
    context, residual_in, out_weight, out_bias, norm_gain, norm_bias, gate_weight, up_weight
):
    me = lax.axis_index("tensor")
    y, z = me // RING, me % RING

    def start_of(other, dz):
        return (jnp.bitwise_xor(y, other) * RING + lax.rem(z + dz + RING, RING)) * ROWS

    def bf(value):
        return value.astype(jnp.bfloat16)

    def f32(value):
        return value.astype(jnp.float32)

    ring = context.reshape(2, RING, ROWS, -1)
    ring = lax.dynamic_slice_in_dim(jnp.concatenate([ring, ring], 1), z, RING, 1)
    ring = jnp.where(y == 0, ring, ring[::-1])

    def product(*blocks):
        rows = [ring[other, dz % RING] for other, dz in blocks]
        rows = jnp.concatenate(rows, 0) if len(rows) > 1 else rows[0]
        return bf(jnp.dot(rows, out_weight, preferred_element_type=jnp.float32))

    far = product((1, 4))
    far, ring = hold((far, ring))
    far = send(far, ACROSS)
    rest = product((1, 1), (1, -1), (1, 3), (1, -3), (1, 2), (1, -2))
    side_up = send(rest[:ROWS], UP)
    side_down = send(rest[ROWS : 2 * ROWS], DOWN)
    three = send(rest[2 * ROWS : 4 * ROWS], ACROSS)
    two = send(rest[4 * ROWS :], ACROSS)
    ring, rest = hold((ring, rest))
    own4, own0, side0 = product((0, 4)), product((0, 0)), product((1, 0))
    own3, own2, own1 = (product((0, dz), (0, -dz)) for dz in (3, 2, 1))

    far, own4, own3, own2, own1, own0, side0 = hold((far, own4, own3, own2, own1, own0, side0))
    total = bf(f32(own4) + f32(far))
    up, down = send(total[:HALF], UP), send(total[HALF:], DOWN)

    up, down, three, side_up, side_down, own3, side0 = hold(
        (up, down, three, side_up, side_down, own3, side0)
    )
    pad = jnp.zeros((HALF, up.shape[1]), jnp.bfloat16)
    own3 = f32(own3) + f32(three)
    up = send(bf(own3[:ROWS] + f32(jnp.concatenate([up, pad], 0))), UP)
    down = send(bf(own3[ROWS:] + f32(jnp.concatenate([pad, down], 0))), DOWN)
    side = send(bf(f32(side0) + f32(side_up) + f32(side_down)), ACROSS)

    up, down, two, own2 = hold((up, down, two, own2))
    own2 = f32(own2) + f32(two)
    up = send(bf(own2[:ROWS] + f32(up)), UP)
    down = send(bf(own2[ROWS:] + f32(down)), DOWN)

    up, down, own1 = hold((up, down, own1))
    up = send(bf(f32(own1[:ROWS]) + f32(up)), UP)
    down = send(bf(f32(own1[ROWS:]) + f32(down)), DOWN)

    attended = f32(own0) + f32(side) + f32(up) + f32(down)

    stream = f32(residual_in) + attended + out_bias
    center = jnp.mean(stream, axis=1, keepdims=True)
    spread = jnp.mean((stream - center) ** 2, axis=1, keepdims=True)
    normed = bf((stream - center) / jnp.sqrt(spread + 1e-05) * norm_gain + norm_bias)

    hidden = jnp.zeros((context.shape[0], gate_weight.shape[1]), jnp.bfloat16)

    def units(hidden, blocks):
        rows = jnp.concatenate([rows for rows, _ in blocks], 0)
        gate = jnp.dot(rows, gate_weight, preferred_element_type=jnp.float32)
        up = jnp.dot(rows, up_weight, preferred_element_type=jnp.float32)
        out = bf(jax.nn.gelu(gate, approximate=False) * up)
        for i, (_, block) in enumerate(blocks):
            hidden = lax.dynamic_update_slice_in_dim(
                hidden, out[i * ROWS : (i + 1) * ROWS], start_of(*block), 0
            )
        return hidden

    up1, down1 = send(normed, UP), send(normed, DOWN)
    other = send(normed, ACROSS)
    up1, down1, other, normed = hold((up1, down1, other, normed))

    up2, down2 = send(up1, UP), send(down1, DOWN)
    side_up1, side_down1 = send(other, UP), send(other, DOWN)
    up2, down2, up1, down1, other, normed = hold((up2, down2, up1, down1, other, normed))

    up3, down3 = send(up2, UP), send(down2, DOWN)
    two = send(jnp.concatenate([up2, down2], 0), ACROSS)
    hidden = units(
        hidden, [(normed, (0, 0)), (other, (1, 0)), (up1, (0, -1)), (down1, (0, 1))]
    )
    up3, down3, side_up1, side_down1, up2, down2, hidden, normed = hold(
        (up3, down3, side_up1, side_down1, up2, down2, hidden, normed)
    )

    up4, down4 = send(up3[:HALF], UP), send(down3[HALF:], DOWN)
    up4, down4, two, up2, hidden = hold((up4, down4, two, up2, hidden))

    four = jnp.concatenate([up4, down4], 0)
    other_four = send(four, ACROSS)
    side_up3, side_down3 = send(two[:ROWS], UP), send(two[ROWS:], DOWN)
    hidden = units(
        hidden, [(side_up1, (1, -1)), (side_down1, (1, 1)), (up2, (0, -2)), (down2, (0, 2))]
    )
    hidden = units(
        hidden, [(two[:ROWS], (1, -2)), (two[ROWS:], (1, 2)), (up3, (0, -3)), (down3, (0, 3))]
    )
    hidden = units(
        hidden, [(side_up3, (1, -3)), (side_down3, (1, 3)), (four, (0, 4)), (other_four, (1, 4))]
    )
    return (normed, hidden)


def solution(mesh):
    in_specs = (
        P("dp", "tensor"),
        P(("dp", "tensor"), None),
        P("tensor", None),
        P(),
        P(),
        P(),
        P(None, "tensor"),
        P(None, "tensor"),
    )
    out_specs = (P(("dp", "tensor"), None), P("dp", "tensor"))
    return jax.shard_map(shards, mesh=mesh, in_specs=in_specs, out_specs=out_specs, check_vma=False)
```

```python
import jax
import jax.numpy as jnp
from jax import lax
from jax.sharding import PartitionSpec as P

ROWS = 32
RING = 8
HALF = ROWS // 2


def index_of(y, z):
    return (y % 2) * RING + z % RING


def ring_pairs(step):
    return [(index_of(y, z), index_of(y, z + step)) for y in range(2) for z in range(RING)]


UP, DOWN = ring_pairs(1), ring_pairs(-1)
ACROSS = [(index_of(y, z), index_of(y + 1, z)) for y in range(2) for z in range(RING)]


def send(value, pairs):
    return lax.ppermute(value, "tensor", pairs)


def hold(values):
    return lax.optimization_barrier(values)


def shards(
    context, residual_in, out_weight, out_bias, norm_gain, norm_bias, gate_weight, up_weight
):
    me = lax.axis_index("tensor")
    y, z = me // RING, me % RING

    def start_of(other, dz):
        return (jnp.bitwise_xor(y, other) * RING + lax.rem(z + dz + RING, RING)) * ROWS

    def bf(value):
        return value.astype(jnp.bfloat16)

    def f32(value):
        return value.astype(jnp.float32)

    ring = context.reshape(2, RING, ROWS, -1)
    ring = lax.dynamic_slice_in_dim(jnp.concatenate([ring, ring], 1), z, RING, 1)
    ring = jnp.where(y == 0, ring, ring[::-1])

    def product(*blocks):
        rows = [ring[other, dz % RING] for other, dz in blocks]
        rows = jnp.concatenate(rows, 0) if len(rows) > 1 else rows[0]
        return bf(jnp.dot(rows, out_weight, preferred_element_type=jnp.float32))

    far = product((1, 4))
    far, ring = hold((far, ring))
    far = send(far, ACROSS)
    rest = product((1, 2), (1, -2), (1, 3), (1, -3))
    side_up = send(rest[:ROWS], UP)
    side_down = send(rest[ROWS : 2 * ROWS], DOWN)
    three = send(rest[2 * ROWS :], ACROSS)
    ring, rest = hold((ring, rest))
    own4, own0, side1, side0 = (
        product((0, 4)), product((0, 0)), product((1, 1), (1, -1)), product((1, 0))
    )
    own3, own2, own1 = (product((0, dz), (0, -dz)) for dz in (3, 2, 1))

    far, own4, own3, own2, own1, own0, side1, side0 = hold(
        (far, own4, own3, own2, own1, own0, side1, side0)
    )
    total = bf(f32(own4) + f32(far))
    up, down = send(total[:HALF], UP), send(total[HALF:], DOWN)

    up, down, three, side_up, side_down, own3, side1, side0 = hold(
        (up, down, three, side_up, side_down, own3, side1, side0)
    )
    one = send(bf(f32(side1) + jnp.concatenate([f32(side_up), f32(side_down)], 0)), ACROSS)
    pad = jnp.zeros((HALF, up.shape[1]), jnp.bfloat16)
    own3 = f32(own3) + f32(three)
    up = send(bf(own3[:ROWS] + f32(jnp.concatenate([up, pad], 0))), UP)
    down = send(bf(own3[ROWS:] + f32(jnp.concatenate([pad, down], 0))), DOWN)

    up, down, own2, side0 = hold((up, down, own2, side0))
    zero = send(side0, ACROSS)
    up = send(bf(f32(own2[:ROWS]) + f32(up)), UP)
    down = send(bf(f32(own2[ROWS:]) + f32(down)), DOWN)

    up, down, own1, one = hold((up, down, own1, one))
    own1 = f32(own1) + f32(one)
    up = send(bf(own1[:ROWS] + f32(up)), UP)
    down = send(bf(own1[ROWS:] + f32(down)), DOWN)

    attended = f32(own0) + f32(zero) + f32(up) + f32(down)

    stream = f32(residual_in) + attended + out_bias
    center = jnp.mean(stream, axis=1, keepdims=True)
    spread = jnp.mean((stream - center) ** 2, axis=1, keepdims=True)
    normed = bf((stream - center) / jnp.sqrt(spread + 1e-05) * norm_gain + norm_bias)

    hidden = jnp.zeros((context.shape[0], gate_weight.shape[1]), jnp.bfloat16)

    def units(hidden, blocks):
        rows = jnp.concatenate([rows for rows, _ in blocks], 0)
        gate = jnp.dot(rows, gate_weight, preferred_element_type=jnp.float32)
        up = jnp.dot(rows, up_weight, preferred_element_type=jnp.float32)
        out = bf(jax.nn.gelu(gate, approximate=False) * up)
        for i, (_, block) in enumerate(blocks):
            hidden = lax.dynamic_update_slice_in_dim(
                hidden, out[i * ROWS : (i + 1) * ROWS], start_of(*block), 0
            )
        return hidden

    up1, down1 = send(normed, UP), send(normed, DOWN)
    other = send(normed, ACROSS)
    up1, down1, other, normed = hold((up1, down1, other, normed))

    up2, down2 = send(up1, UP), send(down1, DOWN)
    side_up1, side_down1 = send(other, UP), send(other, DOWN)
    up2, down2, up1, down1, other, normed = hold((up2, down2, up1, down1, other, normed))

    up3, down3 = send(up2, UP), send(down2, DOWN)
    two = send(jnp.concatenate([up2, down2], 0), ACROSS)
    hidden = units(
        hidden, [(normed, (0, 0)), (other, (1, 0)), (up1, (0, -1)), (down1, (0, 1))]
    )
    up3, down3, side_up1, side_down1, up2, down2, hidden, normed = hold(
        (up3, down3, side_up1, side_down1, up2, down2, hidden, normed)
    )

    up4, down4 = send(up3[:HALF], UP), send(down3[HALF:], DOWN)
    up4, down4, two, up2, hidden = hold((up4, down4, two, up2, hidden))

    four = jnp.concatenate([up4, down4], 0)
    other_four = send(four, ACROSS)
    side_up3, side_down3 = send(two[:ROWS], UP), send(two[ROWS:], DOWN)
    hidden = units(
        hidden, [(side_up1, (1, -1)), (side_down1, (1, 1)), (up2, (0, -2)), (down2, (0, 2))]
    )
    hidden = units(
        hidden, [(two[:ROWS], (1, -2)), (two[ROWS:], (1, 2)), (up3, (0, -3)), (down3, (0, 3))]
    )
    hidden = units(
        hidden, [(side_up3, (1, -3)), (side_down3, (1, 3)), (four, (0, 4)), (other_four, (1, 4))]
    )
    return (normed, hidden)


def solution(mesh):
    in_specs = (
        P("dp", "tensor"),
        P(("dp", "tensor"), None),
        P("tensor", None),
        P(),
        P(),
        P(),
        P(None, "tensor"),
        P(None, "tensor"),
    )
    out_specs = (P(("dp", "tensor"), None), P("dp", "tensor"))
    return jax.shard_map(shards, mesh=mesh, in_specs=in_specs, out_specs=out_specs, check_vma=False)
```

```python
import jax
import jax.numpy as jnp
from jax import lax
from jax.sharding import PartitionSpec as P

ROWS = 32
RING = 8
HALF = ROWS // 2


def index_of(y, z):
    return (y % 2) * RING + z % RING


def ring_pairs(step):
    return [(index_of(y, z), index_of(y, z + step)) for y in range(2) for z in range(RING)]


UP, DOWN = ring_pairs(1), ring_pairs(-1)
ACROSS = [(index_of(y, z), index_of(y + 1, z)) for y in range(2) for z in range(RING)]


def send(value, pairs):
    return lax.ppermute(value, "tensor", pairs)


def hold(values):
    return lax.optimization_barrier(values)


def shards(
    context, residual_in, out_weight, out_bias, norm_gain, norm_bias, gate_weight, up_weight
):
    me = lax.axis_index("tensor")
    y, z = me // RING, me % RING

    def start_of(other, dz):
        return (jnp.bitwise_xor(y, other) * RING + lax.rem(z + dz + RING, RING)) * ROWS

    def bf(value):
        return value.astype(jnp.bfloat16)

    def f32(value):
        return value.astype(jnp.float32)

    ring = context.reshape(2, RING, ROWS, -1)
    ring = lax.dynamic_slice_in_dim(jnp.concatenate([ring, ring], 1), z, RING, 1)
    ring = jnp.where(y == 0, ring, ring[::-1])

    def product(*blocks):
        rows = [ring[other, dz % RING] for other, dz in blocks]
        rows = jnp.concatenate(rows, 0) if len(rows) > 1 else rows[0]
        return bf(jnp.dot(rows, out_weight, preferred_element_type=jnp.float32))

    far = product((1, 4))
    far, ring = hold((far, ring))
    far = send(far, ACROSS)
    rest = product((1, 2), (1, -2), (1, 3), (1, -3))
    side_up = send(rest[:ROWS], UP)
    side_down = send(rest[ROWS : 2 * ROWS], DOWN)
    three = send(rest[2 * ROWS :], ACROSS)
    ring, rest = hold((ring, rest))
    own4 = product((0, 4))
    far, own4, ring = hold((far, own4, ring))
    total = bf(f32(own4) + f32(far))
    up, down = send(total[:HALF], UP), send(total[HALF:], DOWN)
    own0, side1, side0 = product((0, 0)), product((1, 1), (1, -1)), product((1, 0))
    own3, own2, own1 = (product((0, dz), (0, -dz)) for dz in (3, 2, 1))

    up, down, three, side_up, side_down, own3, own2, own1, own0, side1, side0 = hold(
        (up, down, three, side_up, side_down, own3, own2, own1, own0, side1, side0)
    )
    one = send(bf(f32(side1) + jnp.concatenate([f32(side_up), f32(side_down)], 0)), ACROSS)
    pad = jnp.zeros((HALF, up.shape[1]), jnp.bfloat16)
    own3 = f32(own3) + f32(three)
    up = send(bf(own3[:ROWS] + f32(jnp.concatenate([up, pad], 0))), UP)
    down = send(bf(own3[ROWS:] + f32(jnp.concatenate([pad, down], 0))), DOWN)

    up, down, own2, side0 = hold((up, down, own2, side0))
    zero = send(side0, ACROSS)
    up = send(bf(f32(own2[:ROWS]) + f32(up)), UP)
    down = send(bf(f32(own2[ROWS:]) + f32(down)), DOWN)

    up, down, own1, one = hold((up, down, own1, one))
    own1 = f32(own1) + f32(one)
    up = send(bf(own1[:ROWS] + f32(up)), UP)
    down = send(bf(own1[ROWS:] + f32(down)), DOWN)

    attended = f32(own0) + f32(zero) + f32(up) + f32(down)

    stream = f32(residual_in) + attended + out_bias
    center = jnp.mean(stream, axis=1, keepdims=True)
    spread = jnp.mean((stream - center) ** 2, axis=1, keepdims=True)
    normed = bf((stream - center) / jnp.sqrt(spread + 1e-05) * norm_gain + norm_bias)

    hidden = jnp.zeros((context.shape[0], gate_weight.shape[1]), jnp.bfloat16)

    def units(hidden, blocks):
        rows = jnp.concatenate([rows for rows, _ in blocks], 0)
        gate = jnp.dot(rows, gate_weight, preferred_element_type=jnp.float32)
        up = jnp.dot(rows, up_weight, preferred_element_type=jnp.float32)
        out = bf(jax.nn.gelu(gate, approximate=False) * up)
        for i, (_, block) in enumerate(blocks):
            hidden = lax.dynamic_update_slice_in_dim(
                hidden, out[i * ROWS : (i + 1) * ROWS], start_of(*block), 0
            )
        return hidden

    up1, down1 = send(normed, UP), send(normed, DOWN)
    other = send(normed, ACROSS)
    up1, down1, other, normed = hold((up1, down1, other, normed))

    up2, down2 = send(up1, UP), send(down1, DOWN)
    side_up1, side_down1 = send(other, UP), send(other, DOWN)
    up2, down2, up1, down1, other, normed = hold((up2, down2, up1, down1, other, normed))

    up3, down3 = send(up2, UP), send(down2, DOWN)
    two = send(jnp.concatenate([up2, down2], 0), ACROSS)
    hidden = units(
        hidden, [(normed, (0, 0)), (other, (1, 0)), (up1, (0, -1)), (down1, (0, 1))]
    )
    up3, down3, side_up1, side_down1, up2, down2, hidden, normed = hold(
        (up3, down3, side_up1, side_down1, up2, down2, hidden, normed)
    )

    up4, down4 = send(up3[:HALF], UP), send(down3[HALF:], DOWN)
    up4, down4, two, up2, hidden = hold((up4, down4, two, up2, hidden))

    four = jnp.concatenate([up4, down4], 0)
    other_four = send(four, ACROSS)
    side_up3, side_down3 = send(two[:ROWS], UP), send(two[ROWS:], DOWN)
    hidden = units(
        hidden, [(side_up1, (1, -1)), (side_down1, (1, 1)), (up2, (0, -2)), (down2, (0, 2))]
    )
    hidden = units(
        hidden, [(two[:ROWS], (1, -2)), (two[ROWS:], (1, 2)), (up3, (0, -3)), (down3, (0, 3))]
    )
    hidden = units(
        hidden, [(side_up3, (1, -3)), (side_down3, (1, 3)), (four, (0, 4)), (other_four, (1, 4))]
    )
    return (normed, hidden)


def solution(mesh):
    in_specs = (
        P("dp", "tensor"),
        P(("dp", "tensor"), None),
        P("tensor", None),
        P(),
        P(),
        P(),
        P(None, "tensor"),
        P(None, "tensor"),
    )
    out_specs = (P(("dp", "tensor"), None), P("dp", "tensor"))
    return jax.shard_map(shards, mesh=mesh, in_specs=in_specs, out_specs=out_specs, check_vma=False)
```

```python
import jax
import jax.numpy as jnp
from jax import lax
from jax.sharding import PartitionSpec as P

ROWS = 32
RING = 8
HALF = ROWS // 2


def index_of(y, z):
    return (y % 2) * RING + z % RING


def ring_pairs(step):
    return [(index_of(y, z), index_of(y, z + step)) for y in range(2) for z in range(RING)]


UP, DOWN = ring_pairs(1), ring_pairs(-1)
ACROSS = [(index_of(y, z), index_of(y + 1, z)) for y in range(2) for z in range(RING)]


def send(value, pairs):
    return lax.ppermute(value, "tensor", pairs)


def hold(values):
    return lax.optimization_barrier(values)


def shards(
    context, residual_in, out_weight, out_bias, norm_gain, norm_bias, gate_weight, up_weight
):
    me = lax.axis_index("tensor")
    y, z = me // RING, me % RING

    def start_of(other, dz):
        return (jnp.bitwise_xor(y, other) * RING + lax.rem(z + dz + RING, RING)) * ROWS

    def bf(value):
        return value.astype(jnp.bfloat16)

    def f32(value):
        return value.astype(jnp.float32)

    ring = context.reshape(2, RING, ROWS, -1)
    ring = lax.dynamic_slice_in_dim(jnp.concatenate([ring, ring], 1), z, RING, 1)
    ring = jnp.where(y == 0, ring, ring[::-1])

    def product(*blocks):
        rows = [ring[other, dz % RING] for other, dz in blocks]
        rows = jnp.concatenate(rows, 0) if len(rows) > 1 else rows[0]
        return bf(jnp.dot(rows, out_weight, preferred_element_type=jnp.float32))

    far = product((1, 4))
    far, ring = hold((far, ring))
    far = send(far, ACROSS)
    rest = product((1, 2), (1, -2), (1, 3), (1, -3))
    side_up = send(rest[:ROWS], UP)
    side_down = send(rest[ROWS : 2 * ROWS], DOWN)
    three = send(rest[2 * ROWS :], ACROSS)
    ring, rest = hold((ring, rest))
    own4 = product((0, 4))
    far, own4, ring = hold((far, own4, ring))
    total = bf(f32(own4) + f32(far))
    up, down = send(total[:HALF], UP), send(total[HALF:], DOWN)
    own0, side1, side0 = product((0, 0)), product((1, 1), (1, -1)), product((1, 0))
    own3, own2, own1 = (product((0, dz), (0, -dz)) for dz in (3, 2, 1))

    up, down, three, side_up, side_down, own3, own2, own1, own0, side1, side0 = hold(
        (up, down, three, side_up, side_down, own3, own2, own1, own0, side1, side0)
    )
    one = send(bf(f32(side1) + jnp.concatenate([f32(side_up), f32(side_down)], 0)), ACROSS)
    pad = jnp.zeros((HALF, up.shape[1]), jnp.bfloat16)
    own3 = f32(own3) + f32(three)
    up = send(bf(own3[:ROWS] + f32(jnp.concatenate([up, pad], 0))), UP)
    down = send(bf(own3[ROWS:] + f32(jnp.concatenate([pad, down], 0))), DOWN)

    up, down, own2, side0 = hold((up, down, own2, side0))
    zero = send(side0, ACROSS)
    up = send(bf(f32(own2[:ROWS]) + f32(up)), UP)
    down = send(bf(f32(own2[ROWS:]) + f32(down)), DOWN)

    up, down, own1, one = hold((up, down, own1, one))
    own1 = f32(own1) + f32(one)
    up = send(bf(own1[:ROWS] + f32(up)), UP)
    down = send(bf(own1[ROWS:] + f32(down)), DOWN)

    attended = f32(own0) + f32(zero) + f32(up) + f32(down)

    stream = f32(residual_in) + attended + out_bias
    center = jnp.mean(stream, axis=1, keepdims=True)
    spread = jnp.mean((stream - center) ** 2, axis=1, keepdims=True)
    normed = bf((stream - center) / jnp.sqrt(spread + 1e-05) * norm_gain + norm_bias)

    hidden = jnp.zeros((context.shape[0], gate_weight.shape[1]), jnp.bfloat16)

    def units(hidden, blocks):
        rows = jnp.concatenate([rows for rows, _ in blocks], 0)
        gate = jnp.dot(rows, gate_weight, preferred_element_type=jnp.float32)
        up = jnp.dot(rows, up_weight, preferred_element_type=jnp.float32)
        out = bf(jax.nn.gelu(gate, approximate=False) * up)
        for i, (_, block) in enumerate(blocks):
            hidden = lax.dynamic_update_slice_in_dim(
                hidden, out[i * ROWS : (i + 1) * ROWS], start_of(*block), 0
            )
        return hidden

    up1, down1 = send(normed, UP), send(normed, DOWN)
    other = send(normed, ACROSS)
    up1, down1, normed = hold((up1, down1, normed))

    up2, down2 = send(up1, UP), send(down1, DOWN)
    side_up1, side_down1 = send(other, UP), send(other, DOWN)
    up2, down2, up1, down1, other, normed = hold((up2, down2, up1, down1, other, normed))

    up3, down3 = send(up2, UP), send(down2, DOWN)
    two = send(jnp.concatenate([up2, down2], 0), ACROSS)
    hidden = units(
        hidden, [(normed, (0, 0)), (other, (1, 0)), (up1, (0, -1)), (down1, (0, 1))]
    )
    up3, down3, side_up1, side_down1, up2, down2, hidden, normed = hold(
        (up3, down3, side_up1, side_down1, up2, down2, hidden, normed)
    )

    up4, down4 = send(up3[:HALF], UP), send(down3[HALF:], DOWN)
    up4, down4, two, up2, hidden = hold((up4, down4, two, up2, hidden))

    four = jnp.concatenate([up4, down4], 0)
    other_four = send(four, ACROSS)
    side_up3, side_down3 = send(two[:ROWS], UP), send(two[ROWS:], DOWN)
    hidden = units(
        hidden, [(side_up1, (1, -1)), (side_down1, (1, 1)), (up2, (0, -2)), (down2, (0, 2))]
    )
    hidden = units(
        hidden, [(two[:ROWS], (1, -2)), (two[ROWS:], (1, 2)), (up3, (0, -3)), (down3, (0, 3))]
    )
    hidden = units(
        hidden, [(side_up3, (1, -3)), (side_down3, (1, 3)), (four, (0, 4)), (other_four, (1, 4))]
    )
    return (normed, hidden)


def solution(mesh):
    in_specs = (
        P("dp", "tensor"),
        P(("dp", "tensor"), None),
        P("tensor", None),
        P(),
        P(),
        P(),
        P(None, "tensor"),
        P(None, "tensor"),
    )
    out_specs = (P(("dp", "tensor"), None), P("dp", "tensor"))
    return jax.shard_map(shards, mesh=mesh, in_specs=in_specs, out_specs=out_specs, check_vma=False)
```
